256 devices in a mesh: tm: 4 (over x), row: 8 (over z), col: 8 (over y, core).
Axes of the slice: x: 4, y: 4, z: 8, core: 2. Of those that a mesh axis runs over, the one named last changes fastest.
Arguments:
- latents: bfloat16 [8, 128, 128, 256], P('tm', 'row', 'col'), may hold values from -33 to 33
- gain_one: float32 [256], replicated, may hold values from 0.1 to 1.9
- shift_one: float32 [256], replicated, may hold values from -3 to 3
- kernel_one: bfloat16 [3, 3, 3, 256, 256], replicated, may hold values from -0.078125 to 0.078125
- offset_one: float32 [256], replicated, may hold values from -3 to 3
- gain_two: float32 [256], replicated, may hold values from 0.1 to 1.9
- shift_two: float32 [256], replicated, may hold values from -3 to 3
- kernel_two: bfloat16 [3, 3, 3, 256, 256], replicated, may hold values from -0.078125 to 0.078125
- offset_two: float32 [256], replicated, may hold values from -3 to 3
- kernel_three: bfloat16 [3, 3, 3, 256, 256], replicated, may hold values from -0.078125 to 0.078125
- offset_three: float32 [256], replicated, may hold values from -3 to 3
Outputs:
- decoded: bfloat16 [8, 256, 256, 256], P('tm', 'row', 'col')
The draws below stay inside these ranges and needn't reach their ends.
All inputs are finite; a program needn't handle non-finite values.
Results may differ from the reference program's by a relative error of at most 0.006.
Values may be sent and summed in bfloat16 or wider, within the bound.
No kernel may reach another device: no remote copies, remote signals or barrier semaphores. Data moves between devices by JAX's collectives and lax.ppermute only.
A program may use at most 128 MiB of HBM per device.

```python
import jax
import jax.numpy as jnp
from jax import lax

C = 256
GROUPS = 32
FRAMES = 8
HEIGHT = 128
WIDTH = 128


def varying_factor(key, length):
    fraction = jax.random.uniform(key, (FRAMES, length), jnp.float32, 0.0, 1.0)
    last_frame = jnp.arange(FRAMES, dtype=jnp.int32)[:, None] == FRAMES - 1
    last_place = jnp.arange(length, dtype=jnp.int32)[None, :] == length - 1
    fraction = jnp.where(last_frame & last_place, 0.0, fraction)
    return jnp.exp(-1.4 * fraction)


def draw_latents(key, part):
    key = jax.random.fold_in(key, 11)
    frame_pos = jnp.arange(FRAMES, dtype=jnp.float32) / max(FRAMES - 1, 1)
    row_pos = jnp.arange(HEIGHT, dtype=jnp.float32) / max(HEIGHT - 1, 1)
    col_pos = jnp.arange(WIDTH, dtype=jnp.float32) / max(WIDTH - 1, 1)
    chan_pos = jnp.arange(C, dtype=jnp.float32) / max(C - 1, 1)
    exponent = frame_pos[:, None, None, None] + row_pos[None, :, None, None] + col_pos[None, None, :, None] + chan_pos[None, None, None, :]
    scales = 0.1 * jnp.power(3.0, exponent)
    row_factor = varying_factor(jax.random.fold_in(key, 1), HEIGHT)
    col_factor = varying_factor(jax.random.fold_in(key, 2), WIDTH)
    scales = scales * row_factor[:, :, None, None] * col_factor[:, None, :, None]
    shifted = jax.random.uniform(jax.random.fold_in(key, 3), (FRAMES, HEIGHT), jnp.float32, -0.5, 0.5)
    shape = (FRAMES, HEIGHT, WIDTH, C)
    base = jax.random.truncated_normal(key, -4.0, 4.0, shape, jnp.float32)
    base = jnp.clip(base + shifted[:, :, None, None], -4.0, 4.0)
    return (base * scales).astype(jnp.bfloat16)


def scatter_about(own_key, extent, spread, limit, held_as=jnp.bfloat16):
    return jnp.clip(spread * jax.random.normal(own_key, extent, jnp.float32), -limit, limit).astype(held_as)


def setup_inputs(seed: int = 0) -> dict:
    key_list = jax.random.split(jax.random.key(seed), 12)
    return {
        "latents": draw_latents(jax.random.fold_in(key_list[11], 71), 0),
        "gain_one": jnp.clip(1.0 + 0.18 * jax.random.normal(key_list[1], (C,), jnp.float32), 0.1, 1.9),
        "shift_one": scatter_about(key_list[2], (C,), 0.5, 3.0, jnp.float32),
        "kernel_one": scatter_about(key_list[3], (3, 3, 3, C, C), (27 * C) ** -0.5, 0.078125),
        "offset_one": scatter_about(key_list[4], (C,), 0.5, 3.0, jnp.float32),
        "gain_two": jnp.clip(1.0 + 0.18 * jax.random.normal(key_list[5], (C,), jnp.float32), 0.1, 1.9),
        "shift_two": scatter_about(key_list[6], (C,), 0.5, 3.0, jnp.float32),
        "kernel_two": scatter_about(key_list[7], (3, 3, 3, C, C), (27 * C) ** -0.5, 0.078125),
        "offset_two": scatter_about(key_list[8], (C,), 0.5, 3.0, jnp.float32),
        "kernel_three": scatter_about(key_list[9], (3, 3, 3, C, C), (27 * C) ** -0.5, 0.078125),
        "offset_three": scatter_about(key_list[10], (C,), 0.5, 3.0, jnp.float32),
    }


EPSILON = 1e-06

def group_norm(values, norm_gain, norm_shift):
    shaped = values.reshape(values.shape[0], values.shape[1], values.shape[2], GROUPS, C // GROUPS)
    group_mean = lax.optimization_barrier(jnp.mean(shaped, axis=(0, 1, 2, 4), keepdims=True))
    centered = shaped - group_mean
    group_var = lax.optimization_barrier(jnp.mean(centered * centered, axis=(0, 1, 2, 4), keepdims=True))
    normed = (centered * lax.rsqrt(group_var + EPSILON)).reshape(values.shape)
    return normed * norm_gain + norm_shift

def causal_conv(active, kernel, offset):
    frame_count, row_count, col_count = (active.shape[0], active.shape[1], active.shape[2])
    padded = jnp.concatenate([active[:1], active[:1], active], axis=0)
    padded = jnp.pad(padded, ((0, 0), (1, 1), (1, 1), (0, 0)), mode='edge')
    flat_kernel = kernel.reshape(3, 9 * C, C)

    def one_frame(position):
        accumulated = jnp.zeros((row_count * col_count, C), jnp.float32)
        for time_tap in range(3):
            window = lax.dynamic_index_in_dim(padded, position + time_tap, 0, keepdims=False)
            stacked = jnp.concatenate([window[row_tap:row_tap + row_count, col_tap:col_tap + col_count, :] for row_tap in range(3) for col_tap in range(3)], axis=-1)
            stacked = stacked.reshape(row_count * col_count, 9 * C)
            accumulated = accumulated + jnp.dot(stacked, flat_kernel[time_tap], preferred_element_type=jnp.float32)
        return accumulated.reshape(row_count, col_count, C) + offset
    return lax.map(one_frame, jnp.arange(frame_count, dtype=jnp.int32))

def reference(latents, gain_one, shift_one, kernel_one, offset_one, gain_two, shift_two, kernel_two, offset_two, kernel_three, offset_three):
    act_one = jax.nn.silu(group_norm(latents.astype(jnp.float32), gain_one, shift_one)).astype(jnp.bfloat16)
    hidden = causal_conv(act_one, kernel_one, offset_one)
    act_two = jax.nn.silu(group_norm(hidden, gain_two, shift_two)).astype(jnp.bfloat16)
    block_out = (latents.astype(jnp.float32) + causal_conv(act_two, kernel_two, offset_two)).astype(jnp.bfloat16)
    upsampled = jnp.repeat(jnp.repeat(block_out, 2, axis=1), 2, axis=2)
    return causal_conv(upsampled, kernel_three, offset_three).astype(jnp.bfloat16)
```

```python
import jax
import jax.numpy as jnp
from jax import lax
from jax.sharding import PartitionSpec as P

GROUPS = 32


EPSILON = 1e-06


def shifted(block, axis, distance):
    devices = range(lax.axis_size(axis))
    route = [(i - distance, i) for i in devices if i - distance in devices]
    return lax.ppermute(block, axis, route)


def extended(value, sides, width):
    for axis, dim in sides:
        peers, length = (lax.axis_size(axis), value.shape[dim])
        up = [(i, (i + 1) % peers) for i in range(peers - 1)]
        down = [(j, i) for i, j in up]
        last = lax.slice_in_dim(value, length - width, length, axis=dim)
        initial = lax.slice_in_dim(value, 0, width, axis=dim)
        before = lax.ppermute(last, axis, up)
        after = lax.ppermute(initial, axis, down)
        value = jnp.concatenate([before, value, after], axis=dim)
    return value


def group_stats(values, group_count):
    shaped = values.reshape(-1, group_count, values.shape[3] // group_count)
    count = shaped.shape[0] * shaped.shape[2]
    own_mean = jnp.sum(shaped, axis=(0, 2)) / count
    centered = shaped - own_mean[:, None]
    own_spread = jnp.sum(centered * centered, axis=(0, 2))
    return combine_stats(own_mean, own_spread, count)


def combine_stats(own_mean, own_spread, count):
    group_count = own_mean.shape[0]
    devices = lax.axis_size("tm") * lax.axis_size("row") * lax.axis_size("col")
    row = jnp.concatenate([own_mean, own_spread, own_mean, own_spread])[None]
    sent = jnp.broadcast_to(row, (devices, row.shape[1]))
    every = lax.all_to_all(sent, ("tm", "row", "col"), 0, 0, tiled=True)
    means = every[:, :group_count]
    spreads = every[:, group_count : 2 * group_count]
    mean = jnp.mean(means, axis=0)
    off = means - mean
    spread = jnp.sum(spreads, axis=0) + count * jnp.sum(off * off, axis=0)
    return mean, spread / (count * devices)


def norm_silu(values, norm_gain, norm_shift, group_count):
    group_mean, group_var = group_stats(values, group_count)
    width = values.shape[3] // group_count
    mean = jnp.repeat(group_mean, width)
    scale = jnp.repeat(lax.rsqrt(group_var + EPSILON), width)
    normed = (values - mean) * scale
    return jax.nn.silu(normed * norm_gain + norm_shift).astype(jnp.bfloat16)


def with_past(active, received):
    first_copy = jnp.concatenate([active[:1], active[:1]], axis=0)
    earlier = jnp.where(lax.axis_index("tm") == 0, first_copy, received)
    return jnp.concatenate([earlier, active], axis=0)


def edge_fill(padded):
    row_first = lax.axis_index("row") == 0
    row_last = lax.axis_index("row") == lax.axis_size("row") - 1
    top_rim = jnp.where(row_first, padded[:, 1:2], padded[:, :1])
    bottom_rim = jnp.where(row_last, padded[:, -2:-1], padded[:, -1:])
    padded = jnp.concatenate([top_rim, padded[:, 1:-1], bottom_rim], axis=1)
    col_first = lax.axis_index("col") == 0
    col_last = lax.axis_index("col") == lax.axis_size("col") - 1
    left_rim = jnp.where(col_first, padded[:, :, 1:2], padded[:, :, :1])
    right_rim = jnp.where(col_last, padded[:, :, -2:-1], padded[:, :, -1:])
    return jnp.concatenate([left_rim, padded[:, :, 1:-1], right_rim], axis=2)


def prepare(active):
    received = shifted(active, "tm", 1)
    joined = with_past(active, received)
    return edge_fill(extended(joined, (("row", 1), ("col", 2)), 1))


def conv_local(padded, kernel, offset):
    frame_count = padded.shape[0] - 2
    row_count = padded.shape[1] - 2
    col_count = padded.shape[2] - 2
    channels = padded.shape[3]
    flat_kernel = kernel.reshape(3, 9 * channels, kernel.shape[4])
    accumulated = jnp.zeros((frame_count * row_count * col_count, kernel.shape[4]), jnp.float32)
    for time_tap in range(3):
        window = padded[time_tap : time_tap + frame_count]
        stacked = jnp.concatenate(
            [
                window[:, row_tap : row_tap + row_count, col_tap : col_tap + col_count, :]
                for row_tap in range(3)
                for col_tap in range(3)
            ],
            axis=-1,
        )
        stacked = stacked.reshape(frame_count * row_count * col_count, 9 * channels)
        accumulated = accumulated + jnp.dot(
            stacked, flat_kernel[time_tap], preferred_element_type=jnp.float32
        )
    return accumulated.reshape(frame_count, row_count, col_count, kernel.shape[4]) + offset


def on_device(
    latents,
    gain_one,
    shift_one,
    kernel_one,
    offset_one,
    gain_two,
    shift_two,
    kernel_two,
    offset_two,
    kernel_three,
    offset_three,
):
    act_one = norm_silu(latents.astype(jnp.float32), gain_one, shift_one, GROUPS)
    hidden = conv_local(prepare(act_one), kernel_one, offset_one)
    act_two = norm_silu(hidden, gain_two, shift_two, GROUPS)
    block_out = (
        latents.astype(jnp.float32) + conv_local(prepare(act_two), kernel_two, offset_two)
    ).astype(jnp.bfloat16)
    upsampled = jnp.repeat(jnp.repeat(block_out, 2, axis=1), 2, axis=2)
    received = shifted(upsampled, "tm", 1)
    joined = with_past(upsampled, received)
    padded = edge_fill(extended(joined, (("row", 1), ("col", 2)), 1))
    return conv_local(padded, kernel_three, offset_three).astype(jnp.bfloat16)


def solution(mesh):
    return jax.shard_map(
        on_device,
        mesh=mesh,
        in_specs=(P("tm", "row", "col", None), P(), P(), P(), P(), P(), P(), P(), P(), P(), P()),
        out_specs=P("tm", "row", "col", None),
        check_vma=False,
    )
```

```python
import functools

import jax
import jax.numpy as jnp
from jax import lax
from jax.experimental import pallas as pl
from jax.experimental.pallas import tpu as pltpu
from jax.sharding import PartitionSpec as P

GROUPS = 32
EPSILON = 1e-06
AXES = ("tm", "row", "col")
F32 = jnp.float32
BF16 = jnp.bfloat16
VMEM = pl.BlockSpec(memory_space=pltpu.VMEM)
PITCH = 20


def exact_dot(a, b):
    return jnp.dot(a, b, precision=lax.Precision.HIGHEST, preferred_element_type=F32)


def lane_to_channel(first, channels):
    lane = lax.broadcasted_iota(jnp.int32, (128, channels), 0)
    group = lax.broadcasted_iota(jnp.int32, (128, channels), 1) // (channels // GROUPS)
    return (lane == group + first).astype(F32)


def channel_to_lane(channels):
    lane = lax.broadcasted_iota(jnp.int32, (channels, 128), 1) % GROUPS
    group = lax.broadcasted_iota(jnp.int32, (channels, 128), 0) // (channels // GROUPS)
    return (lane == group).astype(F32)


def own_stats(flat):
    rows, channels = flat.shape
    to_lane = channel_to_lane(channels)
    count = rows * (channels // GROUPS)
    total = jnp.broadcast_to(jnp.sum(flat, axis=0, keepdims=True), (8, channels))
    mean = exact_dot(total, to_lane) / count
    centered = flat - exact_dot(mean, lane_to_channel(0, channels))[:1]
    spread = jnp.broadcast_to(jnp.sum(centered * centered, axis=0, keepdims=True), (8, channels))
    spread = exact_dot(spread, to_lane)
    lane = lax.broadcasted_iota(jnp.int32, mean.shape, 1)
    return jnp.where(lane < GROUPS, mean, spread)[:1]


def norm_terms(every, gain, count):
    devices = every.shape[0]
    channels = gain.shape[1]
    mean = jnp.sum(every, axis=0, keepdims=True) / devices
    off = every - mean
    between = jnp.broadcast_to(jnp.sum(off * off, axis=0, keepdims=True), (8, 128))
    mean = jnp.broadcast_to(mean, (8, 128))
    to_mean = lane_to_channel(0, channels)
    spread = exact_dot(mean, lane_to_channel(GROUPS, channels)) * devices
    spread = spread + exact_dot(between, to_mean) * count
    var = spread / (count * devices)
    return exact_dot(mean, to_mean)[:1], (gain * lax.rsqrt(var[:1] + EPSILON))


def norm_silu(value, mean, factor, shift):
    normed = (value.astype(F32) - mean) * factor + shift
    half = 0.5 * normed
    return half * jnp.tanh(half) + half


def place():
    at = [lax.axis_index(axis) for axis in AXES]
    return (
        at[0],
        at[1] == 0,
        at[1] == lax.axis_size("row") - 1,
        at[2] == 0,
        at[2] == lax.axis_size("col") - 1,
    )


def taps(kernel_ref, p, q):
    return jnp.concatenate([kernel_ref[s, p, q] for s in range(3)], axis=0)


def stats_kernel(latents_ref, sent_ref):
    value = latents_ref[...].astype(F32)
    flat = value.reshape(-1, value.shape[3])
    sent_ref[...] = jnp.broadcast_to(own_stats(flat), sent_ref.shape)


def fill_rows(act_ref, frame, first, body, left, right, terms, halo, edges):
    _, _, _, col_first, col_last = edges
    rows = pl.ds(first, body.shape[0])
    body = body.astype(F32)
    left = jnp.where(col_first, body[:, :1], left.astype(F32))
    right = jnp.where(col_last, body[:, 15:16], right.astype(F32))
    if terms is not None:
        body, left, right = (norm_silu(v, *terms) for v in (body, left, right))
    act_ref[frame, rows, 8:24] = body
    act_ref[frame, rows, 8 - halo : 8] = left
    act_ref[frame, rows, 24 : 24 + halo] = right


def fill_frame(act_ref, frame, pieces, terms, halo, edges):
    body_ref, at, left_ref, right_ref, top_ref, bottom_ref, ct_ref, cb_ref, source = pieces
    _, row_first, row_last, _, _ = edges
    body = body_ref[at]
    left = left_ref[source][:, 3 - halo :]
    right = right_ref[source][:, :halo]
    fill_rows(act_ref, frame, halo, body, left, right, terms, halo, edges)
    corner = ct_ref[source][3 - halo :]
    fill_rows(
        act_ref,
        frame,
        0,
        jnp.where(row_first, body[:1], top_ref[source][3 - halo :]),
        jnp.where(row_first, left[:1], corner[:, 3 - halo : 3]),
        jnp.where(row_first, right[:1], corner[:, 3 : 3 + halo]),
        terms,
        halo,
        edges,
    )
    corner = cb_ref[source][:halo]
    fill_rows(
        act_ref,
        frame,
        halo + 16,
        jnp.where(row_last, body[15:16], bottom_ref[source][:halo]),
        jnp.where(row_last, left[15:16], corner[:, 3 - halo : 3]),
        jnp.where(row_last, right[15:16], corner[:, 3 : 3 + halo]),
        terms,
        halo,
        edges,
    )


def own_kernel(
    every_ref, r1_ref, x_ref, left_ref, right_ref, top_ref, bottom_ref, ct_ref, cb_ref,
    gain_ref, shift_ref, kernel_ref, offset_ref, sent_ref, act_ref,
):
    edges = place()
    count = 512 * (gain_ref.shape[1] // GROUPS)
    terms = (*norm_terms(every_ref[...], gain_ref[...], count), shift_ref[...])
    halos = (left_ref, right_ref, top_ref, bottom_ref, ct_ref, cb_ref)
    for frame in range(4):
        body = (r1_ref, x_ref)[frame // 2]
        fill_frame(act_ref, frame, (body, frame % 2, *halos, frame + 4), terms, 1, edges)
    first = jnp.where(edges[0] == 0, 2, 0)
    total = None
    for p in range(3):
        for q in range(3):
            rows = []
            for frame in range(2):
                parts = [
                    act_ref[jnp.maximum(frame + s, first), p : p + 16, 7 + q : 23 + q]
                    .reshape(256, -1)
                    .astype(BF16)
                    for s in range(3)
                ]
                rows.append(jnp.concatenate(parts, axis=1))
            product = jnp.dot(
                jnp.concatenate(rows, axis=0), taps(kernel_ref, p, q), preferred_element_type=F32
            )
            total = product if total is None else total + product
    hidden = total + offset_ref[...]
    sent_ref[...] = jnp.broadcast_to(own_stats(hidden), sent_ref.shape)


def wide_kernel(
    every_ref, r3_ref, r2_ref, r1_ref, x_ref, left_ref, right_ref, top_ref, bottom_ref, ct_ref, cb_ref,
    gain_ref, shift_ref, kernel_ref, offset_ref, hidden_ref, base_ref, act_ref, held_ref,
):
    edges = place()
    tm, row_first, row_last, col_first, col_last = edges
    count = 512 * (gain_ref.shape[1] // GROUPS)
    terms = (*norm_terms(every_ref[...], gain_ref[...], count), shift_ref[...])
    halos = (left_ref, right_ref, top_ref, bottom_ref, ct_ref, cb_ref)
    bodies = (r3_ref, r2_ref, r1_ref, x_ref)
    for frame in range(4, 8):
        pieces = (bodies[frame // 2], frame % 2, *halos, frame)
        fill_frame(act_ref, 0, pieces, None, 3, edges)
        for row in range(18):
            base_ref[frame - 4, row * PITCH : row * PITCH + 18] = act_ref[0, row + 2, 7:25]
    for frame in range(8):
        pieces = (bodies[frame // 2], frame % 2, *halos, frame)
        fill_frame(act_ref, frame, pieces, terms, 3, edges)
    first = jnp.maximum(6 - 2 * tm, 0)

    def one_frame(frame, carry):
        for p in range(3):
            for q in range(3):
                parts = [
                    act_ref[jnp.maximum(frame + s, first), p : p + 20, 5 + q : 29 + q]
                    .reshape(480, -1)
                    .astype(BF16)
                    for s in range(3)
                ]
                product = jnp.dot(
                    jnp.concatenate(parts, axis=1), taps(kernel_ref, p, q), preferred_element_type=F32
                ).reshape(20, 24, -1)
                if p + q == 0:
                    held_ref[...] = product + offset_ref[...]
                else:
                    held_ref[...] += product

        @pl.when(col_first)
        def _():
            held_ref[:, 0:2] = jnp.broadcast_to(held_ref[:, 2:3], (20, 2, held_ref.shape[2]))

        @pl.when(col_last)
        def _():
            held_ref[:, 18:20] = jnp.broadcast_to(held_ref[:, 17:18], (20, 2, held_ref.shape[2]))

        @pl.when(row_first)
        def _():
            held_ref[0] = held_ref[2]
            held_ref[1] = held_ref[2]

        @pl.when(row_last)
        def _():
            held_ref[18] = held_ref[17]
            held_ref[19] = held_ref[17]

        for row in range(20):
            hidden_ref[frame, row * PITCH : row * PITCH + PITCH] = held_ref[row, 0:PITCH]
        return carry

    lax.fori_loop(0, 6, one_frame, 0)


def last_kernel(
    every_ref, hidden_ref, base_ref, gain_ref, shift_ref, kernel_two_ref, offset_two_ref,
    kernel_three_ref, offset_three_ref, out_ref, act_ref, block_ref, part_ref, sum_ref, mix_ref,
):
    tm, row_first, row_last, col_first, col_last = place()
    channels = gain_ref.shape[1]
    count = 512 * (channels // GROUPS)
    terms = (*norm_terms(every_ref[...], gain_ref[...], count), shift_ref[...])
    for frame in range(6):
        act_ref[frame, 0:400] = norm_silu(hidden_ref[frame, 0:400], *terms)
    first = jnp.maximum(4 - 2 * tm, 0)
    size = 18 * PITCH
    for pair in range(2):
        for p in range(3):
            for q in range(3):
                rows = []
                for frame in (2 * pair, 2 * pair + 1):
                    start = p * PITCH + q
                    parts = [
                        act_ref[jnp.maximum(frame + s, first), start : start + size] for s in range(3)
                    ]
                    rows.append(jnp.concatenate(parts, axis=1))
                product = jnp.dot(
                    jnp.concatenate(rows, axis=0).astype(BF16),
                    taps(kernel_two_ref, p, q),
                    preferred_element_type=F32,
                ).reshape(2, size, channels)
                frames = slice(2 * pair, 2 * pair + 2)
                if p + q == 0:
                    block_ref[frames] = product + (base_ref[frames] + offset_two_ref[...])
                else:
                    block_ref[frames] += product

    @pl.when(col_first)
    def _():
        for frame in range(4):
            for row in range(18):
                at = row * PITCH
                block_ref[frame, at : at + 1] = block_ref[frame, at + 1 : at + 2]

    @pl.when(col_last)
    def _():
        for frame in range(4):
            for row in range(18):
                at = row * PITCH + 17
                block_ref[frame, at : at + 1] = block_ref[frame, at - 1 : at]

    @pl.when(row_first)
    def _():
        for frame in range(4):
            block_ref[frame, 0:PITCH] = block_ref[frame, PITCH : 2 * PITCH]

    @pl.when(row_last)
    def _():
        for frame in range(4):
            block_ref[frame, 17 * PITCH : size] = block_ref[frame, 16 * PITCH : 17 * PITCH]

    first = jnp.where(tm == 0, 2, 0)
    rows = [
        jnp.concatenate([block_ref[jnp.maximum(frame + s, first)] for s in range(3)], axis=1)
        for frame in range(2)
    ]
    wide = jnp.concatenate(rows, axis=0).astype(BF16)
    out_size = 16 * PITCH
    for p in range(3):
        parts = [
            jnp.dot(wide, taps(kernel_three_ref, p, q), preferred_element_type=F32).reshape(
                2, size, channels
            )
            for q in range(3)
        ]
        part_ref[0, :, 0:size] = parts[0]
        part_ref[1, :, 0:size] = parts[1] + parts[2]
        part_ref[2, :, 0:size] = parts[0] + parts[1]
        part_ref[3, :, 0:size] = parts[2]
        for b in range(2):
            column = part_ref[2 * b, :, b : b + size] + part_ref[2 * b + 1, :, b + 1 : b + 1 + size]
            part_ref[4, :, 0:size] = column
            for a in range(2):
                down = PITCH * ((0, 1, 1) if a == 0 else (1, 1, 2))[p]
                term = part_ref[4, :, down : down + out_size]
                if p == 0:
                    sum_ref[a, b] = term + offset_three_ref[...]
                else:
                    sum_ref[a, b] += term
    for frame in range(2):
        for a in range(2):
            for half in range(channels // 128):
                lanes = slice(half * 128, half * 128 + 128)
                for b in range(2):
                    mix_ref[pl.ds(b, out_size, stride=2), :] = sum_ref[a, b, frame, :, lanes]
                for i in range(16):
                    at = 2 * PITCH * i
                    out_ref[frame, 2 * i + a, :, lanes] = mix_ref[at : at + 32].astype(BF16)


def run_kernel(body, name, out_shape, scratch, flops, *args):
    one = not isinstance(out_shape, tuple)
    return pl.pallas_call(
        body,
        name=name,
        out_shape=out_shape,
        in_specs=[VMEM] * len(args),
        out_specs=VMEM if one else (VMEM,) * len(out_shape),
        scratch_shapes=scratch,
        cost_estimate=pl.CostEstimate(flops=flops, bytes_accessed=8 * 2**20, transcendentals=0),
        compiler_params=pltpu.CompilerParams(vmem_limit_bytes=48 * 2**20),
    )(*args)


def every_row(sent):
    return lax.all_to_all(sent, AXES, 0, 0, tiled=True)


def moved(value, axis, distance):
    devices = range(lax.axis_size(axis))
    return lax.ppermute(value, axis, [(i, i + distance) for i in devices if i + distance in devices])


def exchange(x):
    r1, r2, r3 = (moved(x, "tm", d) for d in (1, 2, 3))
    frames = (r3, r2, r1, x)
    left = moved(jnp.concatenate([v[:, :, 13:] for v in frames]), "col", 1)
    right = moved(jnp.concatenate([v[:, :, :3] for v in frames]), "col", -1)
    top = moved(jnp.concatenate([v[:, 13:] for v in frames]), "row", 1)
    bottom = moved(jnp.concatenate([v[:, :3] for v in frames]), "row", -1)
    sides = jnp.concatenate([left, right], axis=2)
    top_corner = moved(sides[:, 13:], "row", 1)
    bottom_corner = moved(sides[:, :3], "row", -1)
    return r3, r2, r1, (left, right, top, bottom, top_corner, bottom_corner)


def on_device(
    latents, gain_one, shift_one, kernel_one, offset_one, gain_two, shift_two, kernel_two, offset_two,
    kernel_three, offset_three,
):
    channels = latents.shape[3]
    devices = lax.axis_size("tm") * lax.axis_size("row") * lax.axis_size("col")
    gain_one, shift_one, offset_one, gain_two, shift_two, offset_two, offset_three = (
        v[None] for v in (gain_one, shift_one, offset_one, gain_two, shift_two, offset_two, offset_three)
    )
    sent_shape = jax.ShapeDtypeStruct((devices, 128), F32)
    macs = 27 * channels * channels
    sent = run_kernel(stats_kernel, "stats", sent_shape, [], 2**20, latents)
    r3, r2, r1, halos = exchange(latents)
    every = every_row(sent)
    ones = (gain_one, shift_one, kernel_one, offset_one)
    sent = run_kernel(
        own_kernel,
        "own",
        sent_shape,
        [pltpu.VMEM((4, 18, 32, channels), F32)],
        2 * 512 * macs,
        every, r1, latents, *halos, *ones,
    )
    hidden, base = run_kernel(
        wide_kernel,
        "wide",
        (
            jax.ShapeDtypeStruct((6, 408, channels), F32),
            jax.ShapeDtypeStruct((4, 18 * PITCH, channels), F32),
        ),
        [pltpu.VMEM((8, 22, 32, channels), F32), pltpu.VMEM((20, 24, channels), F32)],
        2 * 2880 * macs,
        every, r3, r2, r1, latents, *halos, *ones,
    )
    every = every_row(sent)
    return run_kernel(
        last_kernel,
        "last",
        jax.ShapeDtypeStruct((2, 32, 32, channels), BF16),
        [
            pltpu.VMEM((6, 408, channels), F32),
            pltpu.VMEM((4, 18 * PITCH, channels), F32),
            pltpu.VMEM((5, 2, 19 * PITCH, channels), F32),
            pltpu.VMEM((2, 2, 2, 16 * PITCH, channels), F32),
            pltpu.VMEM((32 * PITCH, 128), F32),
        ],
        2 * 2160 * macs,
        every, hidden, base, gain_two, shift_two, kernel_two, offset_two, kernel_three, offset_three,
    )


def solution(mesh):
    return jax.shard_map(
        on_device,
        mesh=mesh,
        in_specs=(P("tm", "row", "col", None), P(), P(), P(), P(), P(), P(), P(), P(), P(), P()),
        out_specs=P("tm", "row", "col", None),
        check_vma=False,
    )
```

```python
import jax
import jax.numpy as jnp
from jax import lax
from jax.experimental import pallas as pl
from jax.experimental.layout import Layout, with_layout_constraint
from jax.experimental.pallas import tpu as pltpu
from jax.sharding import PartitionSpec as P

GROUPS = 32
EPSILON = 1e-06
AXES = ("tm", "row", "col")
F32 = jnp.float32
BF16 = jnp.bfloat16
VMEM = pl.BlockSpec(memory_space=pltpu.VMEM)
ANY = pl.BlockSpec(memory_space=pl.ANY)
WIDE = 22
PITCH = 20


def exact_dot(a, b):
    return jnp.dot(a, b, precision=lax.Precision.HIGHEST, preferred_element_type=F32)


def iotas(shape):
    return lax.broadcasted_iota(jnp.int32, shape, 0), lax.broadcasted_iota(jnp.int32, shape, 1)


def lane_to_channel(first, channels):
    lane, channel = iotas((128, channels))
    return (lane % 64 == channel // (channels // GROUPS) + first).astype(F32)


def channel_to_lane(channels):
    channel, lane = iotas((channels, 128))
    return (lane % GROUPS == channel // (channels // GROUPS)).astype(F32)


def eight(row):
    return jnp.broadcast_to(row, (8, row.shape[1]))


def own_stats(flat):
    rows, channels = flat.shape
    to_lane = channel_to_lane(channels)
    count = rows * (channels // GROUPS)
    mean = exact_dot(eight(jnp.sum(flat, axis=0, keepdims=True)), to_lane) / count
    own_mean = exact_dot(jnp.where(iotas(mean.shape)[1] < 64, mean, 0.0), lane_to_channel(0, channels))
    centered = flat - own_mean[:1]
    spread = exact_dot(eight(jnp.sum(centered * centered, axis=0, keepdims=True)), to_lane)
    return jnp.where(iotas(mean.shape)[1] % 64 < GROUPS, mean, spread)


def norm_terms(every, gain, cells):
    channels = gain.shape[1]
    devices = 2 * every.shape[0]
    count = cells * (channels // GROUPS)
    total = eight(jnp.sum(every, axis=0, keepdims=True))
    source, lane = iotas((128, 128))
    spread_mean = ((source % 64 < GROUPS) & (source % GROUPS == lane % GROUPS)).astype(F32)
    off = every - exact_dot(total, spread_mean)[:1] / devices
    between = eight(jnp.sum(off * off, axis=0, keepdims=True))
    to_mean = lane_to_channel(0, channels)
    spread = exact_dot(total, lane_to_channel(GROUPS, channels)) + exact_dot(between, to_mean) * count
    var = spread / (count * devices)
    mean = exact_dot(total, to_mean) / devices
    return mean[:1], gain * lax.rsqrt(var[:1] + EPSILON)


def norm_silu(value, mean, factor, shift):
    normed = (value.astype(F32) - mean) * factor + shift
    half = 0.5 * normed
    return half * jnp.tanh(half) + half


def place():
    at = [lax.axis_index(axis) for axis in AXES]
    return (
        at[0],
        at[1] == 0,
        at[1] == lax.axis_size("row") - 1,
        at[2] == 0,
        at[2] == lax.axis_size("col") - 1,
    )


def fetch_taps(kernel_ref, held_ref, sems, rows):
    copies = []
    for p in rows:
        for q in range(3):
            copy = pltpu.make_async_copy(kernel_ref.at[:, p, q], held_ref.at[:, p, q], sems.at[3 * p + q])
            copy.start()
            copies.append(copy)
    return copies


def wait_all(copies):
    for copy in copies:
        copy.wait()


def fetch(pairs, sems):
    copies = [pltpu.make_async_copy(a, b, sems.at[i]) for i, (a, b) in enumerate(pairs)]
    for copy in copies:
        copy.start()
    return copies


def taps(kernel_ref, p, q):
    return jnp.concatenate([kernel_ref[s, p, q] for s in range(3)], axis=0)


def first_kernel(latents_ref, row_ref, copy_ref, first_ref, last_ref):
    value = latents_ref[...].astype(F32)
    copy_ref[...] = latents_ref[...]
    first_ref[...] = value[:, :, :1].astype(BF16)
    last_ref[...] = value[:, :, 15:].astype(BF16)
    row_ref[...] = own_stats(value.reshape(-1, value.shape[3]))


def edge_copy(ref, frames, pitch, rows, cols, edges):
    row_first, row_last, col_first, col_last = edges
    height = sum(rows)

    def copy(frame, to, source, size):
        ref[frame, to : to + size] = ref[frame, source : source + size]

    @pl.when(col_first)
    def _():
        for frame in range(frames):
            for row in range(height):
                for c in range(cols[0]):
                    copy(frame, row * pitch + c, row * pitch + cols[0], 1)

    @pl.when(col_last)
    def _():
        for frame in range(frames):
            for row in range(height):
                at = row * pitch + cols[0] + cols[1]
                for c in range(cols[2]):
                    copy(frame, at + c, at - 1, 1)

    @pl.when(row_first)
    def _():
        for frame in range(frames):
            for row in range(rows[0]):
                copy(frame, row * pitch, rows[0] * pitch, pitch)

    @pl.when(row_last)
    def _():
        end = rows[0] + rows[1]
        for frame in range(frames):
            for row in range(end, height):
                copy(frame, row * pitch, (end - 1) * pitch, pitch)


def strip_kernel(
    every_ref, wide_ref, wide1_ref, p2_ref, p3_ref, gain_ref, shift_ref, kernel_ref, offset_ref,
    row_ref, hidden_ref, act_ref,
):
    tm = lax.axis_index("tm")
    channels = gain_ref.shape[1]
    terms = (*norm_terms(every_ref[...], gain_ref[...], 4 * 512), shift_ref[...])
    rows = pl.ds(4 * tm, 10)
    for distance, piece_ref in enumerate((wide_ref.at[:, rows], wide1_ref.at[:, rows], p2_ref, p3_ref)):
        source = lax.rem(tm + 4 - distance, 4)
        for frame in range(2):
            for row in range(10):
                act_ref[2 * source + frame, row * WIDE : row * WIDE + WIDE] = norm_silu(
                    piece_ref[frame, row], *terms
                )
    size = 8 * WIDE
    for p in range(3):
        for pair in range(4):
            for q in range(3):
                start = p * WIDE + q
                rows = []
                for frame in (2 * pair, 2 * pair + 1):
                    parts = [
                        act_ref[max(frame + s - 2, 0), start : start + size].astype(BF16) for s in range(3)
                    ]
                    rows.append(jnp.concatenate(parts, axis=1))
                product = jnp.dot(
                    jnp.concatenate(rows, axis=0), taps(kernel_ref, p, q), preferred_element_type=F32
                ).reshape(2, size, channels)
                frames = slice(2 * pair, 2 * pair + 2)
                if p + q == 0:
                    hidden_ref[frames] = product + offset_ref[...]
                else:
                    hidden_ref[frames] += product
    own = [
        hidden_ref[frame, row * WIDE + 2 : row * WIDE + 18] for frame in range(8) for row in range(2, 6)
    ]
    own = jnp.concatenate(own, axis=0)
    row_ref[...] = own_stats(own)


def cut_kernel(
    given_ref, s0_ref, s1_ref, s2_ref, s3_ref, hidden_ref, cut_ref,
):
    tm, row_first, row_last, col_first, col_last = place()
    channels = hidden_ref.shape[2]
    hidden_ref[...] = given_ref[...]
    edges = (row_first & (tm == 0), row_last & (tm == 3), col_first, col_last)
    edge_copy(hidden_ref, 8, WIDE, (2, 4, 2), (2, 16, 2), edges)
    center = jnp.zeros((1, channels), F32)
    for frame in range(8):
        center = center + jnp.sum(hidden_ref[frame, 2 * WIDE : 6 * WIDE], axis=0, keepdims=True)
    center = center / (8 * 4 * WIDE)
    high = center.astype(BF16).astype(F32)
    low = (center - high).astype(BF16).astype(F32)
    center = high + low
    for frame in range(8):
        cut_ref[frame, 100:101] = high
        cut_ref[frame, 101:102] = low
        cut_ref[frame, 102:104] = jnp.zeros((2, channels), F32)
    for at in range(4):

        @pl.when(tm == at)
        def _(at=at):
            for frame in range(8):
                for row in range(5):
                    first = (at + row) * WIDE
                    cut_ref[frame, row * PITCH : row * PITCH + PITCH] = (
                        hidden_ref[frame, first : first + PITCH] - center
                    )

    for distance, part_ref in enumerate((s0_ref, s1_ref, s2_ref, s3_ref)):
        target = lax.rem(tm + distance, 4)
        parts = [cut_ref[jnp.maximum(2 * target - 4 + g, 0)] for g in range(6)]
        part_ref[...] = jnp.concatenate(parts, axis=0).astype(BF16)


def last_kernel(
    every_ref, s0_ref, s1_ref, s2_ref, s3_ref, far_before_ref, far_wide_ref, gain_ref, shift_ref, far_two_ref,
    offset_two_ref, far_three_ref, offset_three_ref,
    out_ref, act_ref, block_ref, part_ref, sum_ref, mix_ref, piece_ref, before_ref, wide_ref, kernel_two_ref,
    kernel_three_ref, piece_sems, two_sems, three_sems,
):
    tm, row_first, row_last, col_first, col_last = place()
    channels = gain_ref.shape[1]
    pieces = [(ref, piece_ref.at[d]) for d, ref in enumerate((s0_ref, s1_ref, s2_ref, s3_ref))]
    arrivals = fetch([*pieces, (far_before_ref, before_ref), (far_wide_ref, wide_ref)], piece_sems)
    kernels_two = fetch_taps(far_two_ref, kernel_two_ref, two_sems, (0,))
    mean, factor = norm_terms(every_ref[...], gain_ref[...], 4 * 512)
    wait_all(arrivals[:4])
    kernels_two += fetch_taps(far_two_ref, kernel_two_ref, two_sems, (1, 2))
    for source in range(4):
        held = piece_ref[lax.rem(tm + 4 - source, 4)].astype(F32)
        offset = (held[100:101] + held[101:102]) - mean
        for frame in range(6):
            value = held[frame * 104 : frame * 104 + 100] + offset
            act_ref[frame, source * 100 : source * 100 + 100] = norm_silu(value, 0.0, factor, shift_ref[...])
    wait_all(arrivals[4:])
    for frame in range(4):
        for row in range(18):
            own = wide_ref[max(frame - 2, 0), row + 2, 2:22].astype(F32)
            if frame < 2:
                own = jnp.where(tm == 0, own, before_ref[frame, row + 2, 2:22].astype(F32))
            block_ref[frame, row * PITCH : row * PITCH + PITCH] = own
    size = 18 * PITCH
    for p in range(3):
        wait_all(kernels_two[3 * p : 3 * p + 3])
        if p == 0:
            kernels_three = fetch_taps(far_three_ref, kernel_three_ref, three_sems, range(3))
        for pair in range(2):
            for q in range(3):
                rows = []
                for frame in (2 * pair, 2 * pair + 1):
                    start = p * PITCH + q
                    parts = [act_ref[frame + s, start : start + size] for s in range(3)]
                    rows.append(jnp.concatenate(parts, axis=1))
                product = jnp.dot(
                    jnp.concatenate(rows, axis=0).astype(BF16),
                    taps(kernel_two_ref, p, q),
                    preferred_element_type=F32,
                ).reshape(2, size, channels)
                if p + q == 0:
                    product = product + offset_two_ref[...]
                block_ref[2 * pair : 2 * pair + 2] += product
    edge_copy(block_ref, 4, PITCH, (1, 16, 1), (1, 16, 1), (row_first, row_last, col_first, col_last))
    rows = [
        jnp.concatenate([block_ref[frame + s] for s in range(3)], axis=1)
        for frame in range(2)
    ]
    wide = jnp.concatenate(rows, axis=0).astype(BF16)
    out_size = 16 * PITCH
    wait_all(kernels_three)
    for p in range(3):
        for q in range(3):
            part_ref[q, :, 0:size] = jnp.dot(
                wide, taps(kernel_three_ref, p, q), preferred_element_type=F32
            ).reshape(2, size, channels)
        middle = part_ref[1, :, 1 : 1 + size]
        sum_ref[p, 0] = part_ref[0, :, 0:size] + middle + part_ref[2, :, 1 : 1 + size]
        sum_ref[p, 1] = part_ref[0, :, 1 : 1 + size] + middle + part_ref[2, :, 2 : 2 + size]
    for frame in range(2):
        for half in range(channels // 128):
            lanes = slice(half * 128, half * 128 + 128)
            for b in range(2):
                middle = sum_ref[1, b, frame, PITCH : PITCH + out_size, lanes] + offset_three_ref[:, lanes]
                for a in range(2):
                    up = sum_ref[0, b, frame, a * PITCH : a * PITCH + out_size, lanes]
                    down = sum_ref[2, b, frame, (1 + a) * PITCH : (1 + a) * PITCH + out_size, lanes]
                    mix_ref[frame, half, a, pl.ds(b, out_size, stride=2), :] = up + middle + down
            for a in range(2):
                for i in range(16):
                    at = 2 * PITCH * i
                    out_ref[frame, 2 * i + a, :, lanes] = mix_ref[frame, half, a, at : at + 32].astype(BF16)


def run_kernel(body, name, in_specs, out_shape, scratch, flops, limit, *args):
    return pl.pallas_call(
        body,
        name=name,
        out_shape=out_shape,
        in_specs=in_specs,
        out_specs=jax.tree.map(lambda _: VMEM, out_shape),
        scratch_shapes=scratch,
        cost_estimate=pl.CostEstimate(flops=flops, bytes_accessed=8 * 2**20, transcendentals=0),
        compiler_params=pltpu.CompilerParams(vmem_limit_bytes=limit * 2**20),
    )(*args)


def held_taps(channels):
    return pltpu.VMEM((3, 3, 3, channels, channels), BF16)


def strip_call(every, wide, before, strips, gain, shift, kernel, offset):
    channels = wide.shape[3]
    return run_kernel(
        strip_kernel,
        "strip",
        [VMEM] * 9,
        (jax.ShapeDtypeStruct((8, 128), F32), jax.ShapeDtypeStruct((8, 8 * WIDE, channels), F32)),
        [pltpu.VMEM((8, 224, channels), F32)],
        2 * 1408 * 27 * channels * channels,
        24,
        every, wide, before, *strips, gain, shift, kernel, offset,
    )


def cut_call(hidden):
    channels = hidden.shape[2]
    part_shape = jax.ShapeDtypeStruct((624, channels), BF16)
    scratch = [pltpu.VMEM((8, 8 * WIDE, channels), F32), pltpu.VMEM((8, 104, channels), F32)]
    return run_kernel(cut_kernel, "cut", [VMEM], (part_shape,) * 4, scratch, 2**20, 16, hidden)


def last_call(every, parts, before, wide, gain, shift, kernel_two, offset_two, kernel_three, offset_three):
    channels = wide.shape[3]
    macs = 27 * channels * channels
    return run_kernel(
        last_kernel,
        "last",
        [VMEM] + [ANY] * 6 + [VMEM, VMEM, ANY, VMEM, ANY, VMEM],
        jax.ShapeDtypeStruct((2, 32, 32, channels), BF16),
        [
            pltpu.VMEM((6, 408, channels), F32),
            pltpu.VMEM((4, 18 * PITCH, channels), F32),
            pltpu.VMEM((3, 2, 19 * PITCH, channels), F32),
            pltpu.VMEM((3, 2, 2, 18 * PITCH, channels), F32),
            pltpu.VMEM((2, channels // 128, 2, 32 * PITCH, 128), F32),
            pltpu.VMEM((4, 624, channels), BF16),
            pltpu.VMEM((2, 22, WIDE, channels), BF16),
            pltpu.VMEM((2, 22, WIDE, channels), BF16),
            held_taps(channels),
            held_taps(channels),
            pltpu.SemaphoreType.DMA((6,)),
            pltpu.SemaphoreType.DMA((9,)),
            pltpu.SemaphoreType.DMA((9,)),
        ],
        2 * 2160 * macs,
        62,
        every, *parts, before, wide, gain, shift, kernel_two, offset_two, kernel_three, offset_three,
    )


def merged(rows):
    means = jnp.concatenate([row[:, :GROUPS] for row in rows])
    spreads = jnp.concatenate([row[:, GROUPS:] for row in rows])
    mean = jnp.mean(means, axis=0, keepdims=True)
    off = means - mean
    count = 512 * (256 // GROUPS)
    return jnp.concatenate(
        [mean, jnp.sum(spreads, axis=0, keepdims=True) + count * jnp.sum(off * off, axis=0, keepdims=True)],
        axis=1,
    )


def tm_rows(row):
    row = row[:1, :64]
    return [row] + [around(row, "tm", d) for d in (1, 2, 3)]


def repeated(row):
    row = jnp.concatenate([row, row], axis=1)
    peers = lax.axis_size("row") * lax.axis_size("col")
    return jnp.broadcast_to(row, (peers, row.shape[1]))


def exchanged(sent):
    return lax.all_to_all(sent, ("row", "col"), 0, 0, tiled=True)


def moved(value, axis, distance):
    devices = range(lax.axis_size(axis))
    return lax.ppermute(value, axis, [(i, i + distance) for i in devices if i + distance in devices])


def around(value, axis, distance):
    size = lax.axis_size(axis)
    return lax.ppermute(value, axis, [(i, (i + distance) % size) for i in range(size)])


def gathered(latents):
    _, row_first, row_last, col_first, col_last = place()
    left, right = moved(latents[:, :, 13:], "col", 1), moved(latents[:, :, :3], "col", -1)
    row_shape = jax.ShapeDtypeStruct((8, 128), F32)
    x_shape = jax.ShapeDtypeStruct(latents.shape, BF16)
    side_shape = jax.ShapeDtypeStruct((2, 16, 1, latents.shape[3]), BF16)
    row, x, first, last = run_kernel(
        first_kernel, "first", [VMEM], (row_shape, x_shape, side_shape, side_shape), [], 2**20, 8, latents
    )
    row, x, left, right = lax.optimization_barrier((row, x, left, right))
    left = jnp.where(col_first, first, left)
    right = jnp.where(col_last, last, right)
    x = jnp.concatenate([left, x, right], axis=2)
    top, bottom = moved(x[:, 13:], "row", 1), moved(x[:, :3], "row", -1)
    rows, x, top, bottom = lax.optimization_barrier((tm_rows(row), x, top, bottom))
    top = jnp.where(row_first, x[:, :1], top)
    bottom = jnp.where(row_last, x[:, 15:], bottom)
    return lax.optimization_barrier((merged(rows), jnp.concatenate([top, x, bottom], axis=1)))


def laid(value):
    return with_layout_constraint(value, Layout(tuple(range(value.ndim))))


def strip_of(wide, peer):
    return lax.dynamic_slice_in_dim(wide, 4 * peer, 10, axis=1)


def on_device(
    latents, gain_one, shift_one, kernel_one, offset_one, gain_two, shift_two, kernel_two, offset_two,
    kernel_three, offset_three,
):
    gain_one, shift_one, offset_one, gain_two, shift_two, offset_two, offset_three = (
        v[None] for v in (gain_one, shift_one, offset_one, gain_two, shift_two, offset_two, offset_three)
    )
    tm = lax.axis_index("tm")
    row, wide = gathered(latents)
    wide = laid(wide)
    before = laid(around(wide, "tm", 1))
    strips = [around(strip_of(wide, (tm + d) % 4), "tm", d) for d in (2, 3)]
    every = exchanged(repeated(row))
    row, hidden = strip_call(every, wide, before, strips, gain_one, shift_one, kernel_one, offset_one)
    sent = repeated(merged(tm_rows(row)))
    parts = cut_call(hidden)
    parts = [parts[0]] + [around(parts[d], "tm", d) for d in (1, 2, 3)]
    every = exchanged(sent)
    return last_call(
        every, parts, before, wide, gain_two, shift_two, kernel_two, offset_two, kernel_three, offset_three
    )


def solution(mesh):
    return jax.shard_map(
        on_device,
        mesh=mesh,
        in_specs=(P("tm", "row", "col", None), P(), P(), P(), P(), P(), P(), P(), P(), P(), P()),
        out_specs=P("tm", "row", "col", None),
        check_vma=False,
    )
```

```python
import jax
import jax.numpy as jnp
from jax import lax
from jax.experimental import pallas as pl
from jax.experimental.pallas import tpu as pltpu
from jax.sharding import PartitionSpec as P

GROUPS = 32
EPSILON = 1e-06
AXES = ("tm", "row", "col")
F32 = jnp.float32
BF16 = jnp.bfloat16
VMEM = pl.BlockSpec(memory_space=pltpu.VMEM)
ANY = pl.BlockSpec(memory_space=pl.ANY)
WIDE = 22
PITCH = 20


def exact_dot(a, b):
    high = a.astype(BF16)
    rest = a - high.astype(F32)
    middle = rest.astype(BF16)
    low = (rest - middle.astype(F32)).astype(BF16)
    parts = [part.astype(F32) for part in (high, middle, low)]
    stacked = jnp.concatenate([*parts, jnp.zeros_like(a)], axis=0).astype(BF16)
    product = jnp.dot(stacked, b.astype(BF16), preferred_element_type=F32)
    return product[:8] + (product[8:16] + product[16:24])


def iotas(shape):
    return lax.broadcasted_iota(jnp.int32, shape, 0), lax.broadcasted_iota(jnp.int32, shape, 1)


def lane_to_channel(first, channels):
    lane, channel = iotas((128, channels))
    return (lane % 64 == channel // (channels // GROUPS) + first).astype(F32)


def eight(row):
    return jnp.broadcast_to(row, (8, row.shape[1]))


def own_stats(flat):
    rows, channels = flat.shape
    width = channels // GROUPS
    mean = eight(jnp.sum(flat, axis=0, keepdims=True)) / rows
    centered = flat - mean[:1]
    spread = eight(jnp.sum(centered * centered, axis=0, keepdims=True))
    left, right = iotas((channels, channels))
    group_mean = exact_dot(mean, (left // width == right // width).astype(F32)) / width
    off = mean - group_mean
    spread = spread + rows * off * off
    channel, lane = iotas((channels, 128))
    own = (lane % GROUPS == channel // width).astype(F32)
    first = own * (channel % width == 0).astype(F32)
    both = jnp.where(iotas(mean.shape)[0] < 4, group_mean, spread)
    means, spreads = exact_dot(both, first), exact_dot(both, own)
    return jnp.where(iotas(means.shape)[1] % 64 < GROUPS, eight(means[:1]), eight(spreads[7:]))


def norm_terms(every, gain, cells):
    channels = gain.shape[1]
    devices = 2 * every.shape[0]
    count = cells * (channels // GROUPS)
    total = eight(jnp.sum(every, axis=0, keepdims=True))
    source, lane = iotas((128, 128))
    spread_mean = ((source % 64 < GROUPS) & (source % GROUPS == lane % GROUPS)).astype(F32)
    off = every - exact_dot(total, spread_mean)[:1] / devices
    between = eight(jnp.sum(off * off, axis=0, keepdims=True))
    to_mean = lane_to_channel(0, channels)
    spread = exact_dot(total, lane_to_channel(GROUPS, channels)) + exact_dot(between, to_mean) * count
    var = spread / (count * devices)
    mean = exact_dot(total, to_mean) / devices
    return mean[:1], gain * lax.rsqrt(var[:1] + EPSILON)


def norm_silu(value, mean, factor, shift):
    normed = (value.astype(F32) - mean) * factor + shift
    half = 0.5 * normed
    return half * jnp.tanh(half) + half


def place():
    at = [lax.axis_index(axis) for axis in AXES]
    return (
        at[0],
        at[1] == 0,
        at[1] == lax.axis_size("row") - 1,
        at[2] == 0,
        at[2] == lax.axis_size("col") - 1,
    )


def fetch_taps(kernel_ref, held_ref, sems, rows):
    copies = []
    for p in rows:
        for q in range(3):
            copy = pltpu.make_async_copy(kernel_ref.at[:, p, q], held_ref.at[:, p, q], sems.at[3 * p + q])
            copy.start()
            copies.append(copy)
    return copies


def wait_all(copies):
    for copy in copies:
        copy.wait()


def fetch(pairs, sems):
    copies = [pltpu.make_async_copy(a, b, sems.at[i]) for i, (a, b) in enumerate(pairs)]
    for copy in copies:
        copy.start()
    return copies


def taps(kernel_ref, p, q):
    return jnp.concatenate([kernel_ref[s, p, q] for s in range(3)], axis=0)


def first_kernel(latents_ref, row_ref, copy_ref, first_ref, last_ref):
    value = latents_ref[...].astype(F32)
    copy_ref[...] = latents_ref[...]
    first_ref[...] = value[:, :, :1].astype(BF16)
    last_ref[...] = value[:, :, 15:].astype(BF16)
    row_ref[...] = own_stats(value.reshape(-1, value.shape[3]))


def edge_copy(ref, frames, pitch, rows, cols, edges):
    row_first, row_last, col_first, col_last = edges
    height = sum(rows)

    def copy(frame, to, source, size):
        ref[frame, to : to + size] = ref[frame, source : source + size]

    @pl.when(col_first)
    def _():
        for frame in range(frames):
            for row in range(height):
                for c in range(cols[0]):
                    copy(frame, row * pitch + c, row * pitch + cols[0], 1)

    @pl.when(col_last)
    def _():
        for frame in range(frames):
            for row in range(height):
                at = row * pitch + cols[0] + cols[1]
                for c in range(cols[2]):
                    copy(frame, at + c, at - 1, 1)

    @pl.when(row_first)
    def _():
        for frame in range(frames):
            for row in range(rows[0]):
                copy(frame, row * pitch, rows[0] * pitch, pitch)

    @pl.when(row_last)
    def _():
        end = rows[0] + rows[1]
        for frame in range(frames):
            for row in range(end, height):
                copy(frame, row * pitch, (end - 1) * pitch, pitch)


def strip_kernel(
    every_ref, wide_ref, wide1_ref, p2_ref, p3_ref, gain_ref, shift_ref, kernel_ref, offset_ref,
    row_ref, hidden_ref, act_ref,
):
    tm = lax.axis_index("tm")
    channels = gain_ref.shape[1]
    terms = (*norm_terms(every_ref[...], gain_ref[...], 4 * 512), shift_ref[...])
    rows = pl.ds(4 * tm, 10)
    for distance, piece_ref in enumerate((wide_ref.at[:, rows], wide1_ref.at[:, rows], p2_ref, p3_ref)):
        source = lax.rem(tm + 4 - distance, 4)
        for frame in range(2):
            for row in range(10):
                act_ref[2 * source + frame, row * WIDE : row * WIDE + WIDE] = norm_silu(
                    piece_ref[frame, row], *terms
                )
    size = 8 * WIDE
    for p in range(3):
        for pair in range(4):
            for q in range(3):
                start = p * WIDE + q
                rows = []
                for frame in (2 * pair, 2 * pair + 1):
                    parts = [
                        act_ref[max(frame + s - 2, 0), start : start + size].astype(BF16) for s in range(3)
                    ]
                    rows.append(jnp.concatenate(parts, axis=1))
                product = jnp.dot(
                    jnp.concatenate(rows, axis=0), taps(kernel_ref, p, q), preferred_element_type=F32
                ).reshape(2, size, channels)
                frames = slice(2 * pair, 2 * pair + 2)
                if p + q == 0:
                    hidden_ref[frames] = product + offset_ref[...]
                else:
                    hidden_ref[frames] += product
    own = [
        hidden_ref[frame, row * WIDE + 2 : row * WIDE + 18] for frame in range(8) for row in range(2, 6)
    ]
    own = jnp.concatenate(own, axis=0)
    row_ref[...] = own_stats(own)


def cut_kernel(
    given_ref, s0_ref, s1_ref, s2_ref, s3_ref, hidden_ref, cut_ref,
):
    tm, row_first, row_last, col_first, col_last = place()
    channels = hidden_ref.shape[2]
    hidden_ref[...] = given_ref[...]
    edges = (row_first & (tm == 0), row_last & (tm == 3), col_first, col_last)
    edge_copy(hidden_ref, 8, WIDE, (2, 4, 2), (2, 16, 2), edges)
    center = jnp.zeros((1, channels), F32)
    for frame in range(8):
        center = center + jnp.sum(hidden_ref[frame, 2 * WIDE : 6 * WIDE], axis=0, keepdims=True)
    center = center / (8 * 4 * WIDE)
    high = center.astype(BF16).astype(F32)
    low = (center - high).astype(BF16).astype(F32)
    center = high + low
    for frame in range(8):
        cut_ref[frame, 100:101] = high
        cut_ref[frame, 101:102] = low
        cut_ref[frame, 102:104] = jnp.zeros((2, channels), F32)
    for at in range(4):

        @pl.when(tm == at)
        def _(at=at):
            for frame in range(8):
                for row in range(5):
                    first = (at + row) * WIDE
                    cut_ref[frame, row * PITCH : row * PITCH + PITCH] = (
                        hidden_ref[frame, first : first + PITCH] - center
                    )

    for distance, part_ref in enumerate((s0_ref, s1_ref, s2_ref, s3_ref)):
        target = lax.rem(tm + distance, 4)
        parts = [cut_ref[jnp.maximum(2 * target - 4 + g, 0)] for g in range(6)]
        part_ref[...] = jnp.concatenate(parts, axis=0).astype(BF16)


def last_kernel(
    every_ref, s0_ref, s1_ref, s2_ref, s3_ref, far_before_ref, far_wide_ref, gain_ref, shift_ref, far_two_ref,
    offset_two_ref, far_three_ref, offset_three_ref,
    out_ref, act_ref, block_ref, part_ref, sum_ref, mix_ref, piece_ref, before_ref, wide_ref, kernel_two_ref,
    kernel_three_ref, piece_sems, two_sems, three_sems,
):
    tm, row_first, row_last, col_first, col_last = place()
    channels = gain_ref.shape[1]
    pieces = [(ref, piece_ref.at[d]) for d, ref in enumerate((s0_ref, s1_ref, s2_ref, s3_ref))]
    arrivals = fetch([*pieces, (far_before_ref, before_ref), (far_wide_ref, wide_ref)], piece_sems)
    kernels_two = fetch_taps(far_two_ref, kernel_two_ref, two_sems, (0,))
    mean, factor = norm_terms(every_ref[...], gain_ref[...], 4 * 512)
    wait_all(arrivals[:4])
    kernels_two += fetch_taps(far_two_ref, kernel_two_ref, two_sems, (1, 2))
    for source in range(4):
        held = piece_ref[lax.rem(tm + 4 - source, 4)].astype(F32)
        offset = (held[100:101] + held[101:102]) - mean
        for frame in range(6):
            value = held[frame * 104 : frame * 104 + 100] + offset
            act_ref[frame, source * 100 : source * 100 + 100] = norm_silu(value, 0.0, factor, shift_ref[...])
    wait_all(arrivals[4:])
    for frame in range(4):
        for row in range(18):
            own = wide_ref[max(frame - 2, 0), row + 2, 2:22].astype(F32)
            if frame < 2:
                own = jnp.where(tm == 0, own, before_ref[frame, row + 2, 2:22].astype(F32))
            block_ref[frame, row * PITCH : row * PITCH + PITCH] = own
    size = 18 * PITCH
    for p in range(3):
        wait_all(kernels_two[3 * p : 3 * p + 3])
        if p == 0:
            kernels_three = fetch_taps(far_three_ref, kernel_three_ref, three_sems, range(3))
        for pair in range(2):
            for q in range(3):
                rows = []
                for frame in (2 * pair, 2 * pair + 1):
                    start = p * PITCH + q
                    parts = [act_ref[frame + s, start : start + size] for s in range(3)]
                    rows.append(jnp.concatenate(parts, axis=1))
                product = jnp.dot(
                    jnp.concatenate(rows, axis=0).astype(BF16),
                    taps(kernel_two_ref, p, q),
                    preferred_element_type=F32,
                ).reshape(2, size, channels)
                if p + q == 0:
                    product = product + offset_two_ref[...]
                block_ref[2 * pair : 2 * pair + 2] += product
    edge_copy(block_ref, 4, PITCH, (1, 16, 1), (1, 16, 1), (row_first, row_last, col_first, col_last))
    rows = [
        jnp.concatenate([block_ref[frame + s] for s in range(3)], axis=1)
        for frame in range(2)
    ]
    wide = jnp.concatenate(rows, axis=0).astype(BF16)
    out_size = 16 * PITCH
    wait_all(kernels_three)
    for p in range(3):
        for q in range(3):
            part_ref[q, :, 0:size] = jnp.dot(
                wide, taps(kernel_three_ref, p, q), preferred_element_type=F32
            ).reshape(2, size, channels)
        middle = part_ref[1, :, 1 : 1 + size]
        sum_ref[p, 0] = part_ref[0, :, 0:size] + middle + part_ref[2, :, 1 : 1 + size]
        sum_ref[p, 1] = part_ref[0, :, 1 : 1 + size] + middle + part_ref[2, :, 2 : 2 + size]
    for frame in range(2):
        for half in range(channels // 128):
            lanes = slice(half * 128, half * 128 + 128)
            for b in range(2):
                middle = sum_ref[1, b, frame, PITCH : PITCH + out_size, lanes] + offset_three_ref[:, lanes]
                for a in range(2):
                    up = sum_ref[0, b, frame, a * PITCH : a * PITCH + out_size, lanes]
                    down = sum_ref[2, b, frame, (1 + a) * PITCH : (1 + a) * PITCH + out_size, lanes]
                    mix_ref[frame, half, a, pl.ds(b, out_size, stride=2), :] = up + middle + down
            for a in range(2):
                for i in range(16):
                    at = 2 * PITCH * i
                    out_ref[frame, 2 * i + a, :, lanes] = mix_ref[frame, half, a, at : at + 32].astype(BF16)


def run_kernel(body, name, in_specs, out_shape, scratch, flops, limit, *args):
    return pl.pallas_call(
        body,
        name=name,
        out_shape=out_shape,
        in_specs=in_specs,
        out_specs=jax.tree.map(lambda _: VMEM, out_shape),
        scratch_shapes=scratch,
        cost_estimate=pl.CostEstimate(flops=flops, bytes_accessed=8 * 2**20, transcendentals=0),
        compiler_params=pltpu.CompilerParams(vmem_limit_bytes=limit * 2**20),
    )(*args)


def held_taps(channels):
    return pltpu.VMEM((3, 3, 3, channels, channels), BF16)


def strip_call(every, wide, before, strips, gain, shift, kernel, offset):
    channels = wide.shape[3]
    return run_kernel(
        strip_kernel,
        "strip",
        [VMEM] * 9,
        (jax.ShapeDtypeStruct((8, 128), F32), jax.ShapeDtypeStruct((8, 8 * WIDE, channels), F32)),
        [pltpu.VMEM((8, 224, channels), F32)],
        2 * 1408 * 27 * channels * channels,
        24,
        every, wide, before, *strips, gain, shift, kernel, offset,
    )


def cut_call(hidden):
    channels = hidden.shape[2]
    part_shape = jax.ShapeDtypeStruct((624, channels), BF16)
    scratch = [pltpu.VMEM((8, 8 * WIDE, channels), F32), pltpu.VMEM((8, 104, channels), F32)]
    return run_kernel(cut_kernel, "cut", [VMEM], (part_shape,) * 4, scratch, 2**20, 16, hidden)


def last_call(every, parts, before, wide, gain, shift, kernel_two, offset_two, kernel_three, offset_three):
    channels = wide.shape[3]
    macs = 27 * channels * channels
    return run_kernel(
        last_kernel,
        "last",
        [VMEM] + [ANY] * 6 + [VMEM, VMEM, ANY, VMEM, ANY, VMEM],
        jax.ShapeDtypeStruct((2, 32, 32, channels), BF16),
        [
            pltpu.VMEM((6, 408, channels), F32),
            pltpu.VMEM((4, 18 * PITCH, channels), F32),
            pltpu.VMEM((3, 2, 19 * PITCH, channels), F32),
            pltpu.VMEM((3, 2, 2, 18 * PITCH, channels), F32),
            pltpu.VMEM((2, channels // 128, 2, 32 * PITCH, 128), F32),
            pltpu.VMEM((4, 624, channels), BF16),
            pltpu.VMEM((2, 22, WIDE, channels), BF16),
            pltpu.VMEM((2, 22, WIDE, channels), BF16),
            held_taps(channels),
            held_taps(channels),
            pltpu.SemaphoreType.DMA((6,)),
            pltpu.SemaphoreType.DMA((9,)),
            pltpu.SemaphoreType.DMA((9,)),
        ],
        2 * 2160 * macs,
        62,
        every, *parts, before, wide, gain, shift, kernel_two, offset_two, kernel_three, offset_three,
    )


def merged(rows):
    means = jnp.concatenate([row[:, :GROUPS] for row in rows])
    spreads = jnp.concatenate([row[:, GROUPS:] for row in rows])
    mean = jnp.mean(means, axis=0, keepdims=True)
    off = means - mean
    count = 512 * (256 // GROUPS)
    return jnp.concatenate(
        [mean, jnp.sum(spreads, axis=0, keepdims=True) + count * jnp.sum(off * off, axis=0, keepdims=True)],
        axis=1,
    )


def tm_rows(row):
    row = row[:1, :64]
    return [row] + [around(row, "tm", d) for d in (1, 2, 3)]


def repeated(row):
    row = jnp.concatenate([row, row], axis=1)
    peers = lax.axis_size("row") * lax.axis_size("col")
    return jnp.broadcast_to(row, (peers, row.shape[1]))


def exchanged(sent):
    return lax.all_to_all(sent, ("row", "col"), 0, 0, tiled=True)


def moved(value, axis, distance):
    devices = range(lax.axis_size(axis))
    return lax.ppermute(value, axis, [(i, i + distance) for i in devices if i + distance in devices])


def around(value, axis, distance):
    size = lax.axis_size(axis)
    return lax.ppermute(value, axis, [(i, (i + distance) % size) for i in range(size)])


def gathered(latents):
    _, row_first, row_last, col_first, col_last = place()
    left, right = moved(latents[:, :, 13:], "col", 1), moved(latents[:, :, :3], "col", -1)
    row_shape = jax.ShapeDtypeStruct((8, 128), F32)
    x_shape = jax.ShapeDtypeStruct(latents.shape, BF16)
    side_shape = jax.ShapeDtypeStruct((2, 16, 1, latents.shape[3]), BF16)
    row, x, first, last = run_kernel(
        first_kernel, "first", [VMEM], (row_shape, x_shape, side_shape, side_shape), [], 2**20, 8, latents
    )
    row, x, left, right = lax.optimization_barrier((row, x, left, right))
    left = jnp.where(col_first, first, left)
    right = jnp.where(col_last, last, right)
    x = jnp.concatenate([left, x, right], axis=2)
    top, bottom = moved(x[:, 13:], "row", 1), moved(x[:, :3], "row", -1)
    rows, x, top, bottom = lax.optimization_barrier((tm_rows(row), x, top, bottom))
    top = jnp.where(row_first, x[:, :1], top)
    bottom = jnp.where(row_last, x[:, 15:], bottom)
    return lax.optimization_barrier((merged(rows), jnp.concatenate([top, x, bottom], axis=1)))


def strip_of(wide, peer):
    return lax.dynamic_slice_in_dim(wide, 4 * peer, 10, axis=1)


def on_device(
    latents, gain_one, shift_one, kernel_one, offset_one, gain_two, shift_two, kernel_two, offset_two,
    kernel_three, offset_three,
):
    gain_one, shift_one, offset_one, gain_two, shift_two, offset_two, offset_three = (
        v[None] for v in (gain_one, shift_one, offset_one, gain_two, shift_two, offset_two, offset_three)
    )
    tm = lax.axis_index("tm")
    row, wide = gathered(latents)
    before = around(wide.reshape(44, WIDE, -1), "tm", 1).reshape(wide.shape)
    strips = [around(strip_of(wide, (tm + d) % 4), "tm", d) for d in (2, 3)]
    every = exchanged(repeated(row))
    row, hidden = strip_call(every, wide, before, strips, gain_one, shift_one, kernel_one, offset_one)
    sent = repeated(merged(tm_rows(row)))
    parts = cut_call(hidden)
    parts = [parts[0]] + [around(parts[d], "tm", d) for d in (1, 2, 3)]
    every = exchanged(sent)
    return last_call(
        every, parts, before, wide, gain_two, shift_two, kernel_two, offset_two, kernel_three, offset_three
    )


def solution(mesh):
    return jax.shard_map(
        on_device,
        mesh=mesh,
        in_specs=(P("tm", "row", "col", None), P(), P(), P(), P(), P(), P(), P(), P(), P(), P()),
        out_specs=P("tm", "row", "col", None),
        check_vma=False,
    )
```

```python
import jax
import jax.numpy as jnp
from jax import lax
from jax.experimental import pallas as pl
from jax.experimental.pallas import tpu as pltpu
from jax.sharding import PartitionSpec as P

GROUPS = 32
EPSILON = 1e-06
AXES = ("tm", "row", "col")
F32 = jnp.float32
BF16 = jnp.bfloat16
VMEM = pl.BlockSpec(memory_space=pltpu.VMEM)
ANY = pl.BlockSpec(memory_space=pl.ANY)
WIDE = 22
PITCH = 20


def exact_dot(a, b):
    high = a.astype(BF16)
    rest = a - high.astype(F32)
    middle = rest.astype(BF16)
    low = (rest - middle.astype(F32)).astype(BF16)
    parts = [part.astype(F32) for part in (high, middle, low)]
    stacked = jnp.concatenate([*parts, jnp.zeros_like(a)], axis=0).astype(BF16)
    product = jnp.dot(stacked, b.astype(BF16), preferred_element_type=F32)
    return product[:8] + (product[8:16] + product[16:24])


def iotas(shape):
    return lax.broadcasted_iota(jnp.int32, shape, 0), lax.broadcasted_iota(jnp.int32, shape, 1)


def lane_to_channel(first, channels):
    lane, channel = iotas((128, channels))
    return (lane % 64 == channel // (channels // GROUPS) + first).astype(F32)


def eight(row):
    return jnp.broadcast_to(row, (8, row.shape[1]))


def own_stats(flat):
    rows, channels = flat.shape
    width = channels // GROUPS
    mean = eight(jnp.sum(flat, axis=0, keepdims=True)) / rows
    centered = flat - mean[:1]
    spread = eight(jnp.sum(centered * centered, axis=0, keepdims=True))
    left, right = iotas((channels, channels))
    group_mean = exact_dot(mean, (left // width == right // width).astype(F32)) / width
    off = mean - group_mean
    spread = spread + rows * off * off
    channel, lane = iotas((channels, 128))
    own = (lane % GROUPS == channel // width).astype(F32)
    first = own * (channel % width == 0).astype(F32)
    both = jnp.where(iotas(mean.shape)[0] < 4, group_mean, spread)
    means, spreads = exact_dot(both, first), exact_dot(both, own)
    return jnp.where(iotas(means.shape)[1] % 64 < GROUPS, eight(means[:1]), eight(spreads[7:]))


def norm_terms(every, gain, cells):
    channels = gain.shape[1]
    devices = 2 * every.shape[0]
    count = cells * (channels // GROUPS)
    total = eight(jnp.sum(every, axis=0, keepdims=True))
    source, lane = iotas((128, 128))
    spread_mean = ((source % 64 < GROUPS) & (source % GROUPS == lane % GROUPS)).astype(F32)
    off = every - exact_dot(total, spread_mean)[:1] / devices
    between = eight(jnp.sum(off * off, axis=0, keepdims=True))
    to_mean = lane_to_channel(0, channels)
    spread = exact_dot(total, lane_to_channel(GROUPS, channels)) + exact_dot(between, to_mean) * count
    var = spread / (count * devices)
    mean = exact_dot(total, to_mean) / devices
    return mean[:1], gain * lax.rsqrt(var[:1] + EPSILON)


def norm_silu(value, mean, factor, shift):
    normed = (value.astype(F32) - mean) * factor + shift
    half = 0.5 * normed
    return half * jnp.tanh(half) + half


def place():
    at = [lax.axis_index(axis) for axis in AXES]
    return (
        at[0],
        at[1] == 0,
        at[1] == lax.axis_size("row") - 1,
        at[2] == 0,
        at[2] == lax.axis_size("col") - 1,
    )


def fetch_taps(kernel_ref, held_ref, sems, rows):
    copies = []
    for p in rows:
        for q in range(3):
            copy = pltpu.make_async_copy(kernel_ref.at[:, p, q], held_ref.at[:, p, q], sems.at[3 * p + q])
            copy.start()
            copies.append(copy)
    return copies


def wait_all(copies):
    for copy in copies:
        copy.wait()


def fetch(pairs, sems):
    copies = [pltpu.make_async_copy(a, b, sems.at[i]) for i, (a, b) in enumerate(pairs)]
    for copy in copies:
        copy.start()
    return copies


def taps(kernel_ref, p, q):
    return jnp.concatenate([kernel_ref[s, p, q] for s in range(3)], axis=0)


def first_kernel(latents_ref, row_ref, copy_ref, first_ref, last_ref):
    value = latents_ref[...].astype(F32)
    copy_ref[...] = latents_ref[...]
    first_ref[...] = value[:, :, :1].astype(BF16)
    last_ref[...] = value[:, :, 15:].astype(BF16)
    row_ref[...] = own_stats(value.reshape(-1, value.shape[3]))


def edge_copy(ref, frames, pitch, rows, cols, edges):
    row_first, row_last, col_first, col_last = edges
    height = sum(rows)

    def copy(frame, to, source, size):
        ref[frame, to : to + size] = ref[frame, source : source + size]

    @pl.when(col_first)
    def _():
        for frame in range(frames):
            for row in range(height):
                for c in range(cols[0]):
                    copy(frame, row * pitch + c, row * pitch + cols[0], 1)

    @pl.when(col_last)
    def _():
        for frame in range(frames):
            for row in range(height):
                at = row * pitch + cols[0] + cols[1]
                for c in range(cols[2]):
                    copy(frame, at + c, at - 1, 1)

    @pl.when(row_first)
    def _():
        for frame in range(frames):
            for row in range(rows[0]):
                copy(frame, row * pitch, rows[0] * pitch, pitch)

    @pl.when(row_last)
    def _():
        end = rows[0] + rows[1]
        for frame in range(frames):
            for row in range(end, height):
                copy(frame, row * pitch, (end - 1) * pitch, pitch)


def strip_kernel(
    every_ref, wide_ref, wide1_ref, p2_ref, p3_ref, gain_ref, shift_ref, kernel_ref, offset_ref,
    row_ref, hidden_ref, act_ref,
):
    tm = lax.axis_index("tm")
    channels = gain_ref.shape[1]
    terms = (*norm_terms(every_ref[...], gain_ref[...], 4 * 512), shift_ref[...])
    rows = pl.ds(4 * tm, 10)
    for distance, piece_ref in enumerate((wide_ref.at[:, rows], wide1_ref.at[:, rows], p2_ref, p3_ref)):
        source = lax.rem(tm + 4 - distance, 4)
        for frame in range(2):
            for row in range(10):
                act_ref[2 * source + frame, row * WIDE : row * WIDE + WIDE] = norm_silu(
                    piece_ref[frame, row], *terms
                )
    size = 8 * WIDE
    for p in range(3):
        for pair in range(4):
            for q in range(3):
                start = p * WIDE + q
                rows = []
                for frame in (2 * pair, 2 * pair + 1):
                    parts = [
                        act_ref[max(frame + s - 2, 0), start : start + size].astype(BF16) for s in range(3)
                    ]
                    rows.append(jnp.concatenate(parts, axis=1))
                product = jnp.dot(
                    jnp.concatenate(rows, axis=0), taps(kernel_ref, p, q), preferred_element_type=F32
                ).reshape(2, size, channels)
                frames = slice(2 * pair, 2 * pair + 2)
                if p + q == 0:
                    hidden_ref[frames] = product + offset_ref[...]
                else:
                    hidden_ref[frames] += product
    own = [
        hidden_ref[frame, row * WIDE + 2 : row * WIDE + 18] for frame in range(8) for row in range(2, 6)
    ]
    own = jnp.concatenate(own, axis=0)
    row_ref[...] = own_stats(own)


def cut_kernel(
    given_ref, s0_ref, s1_ref, s2_ref, s3_ref, hidden_ref, cut_ref,
):
    tm, row_first, row_last, col_first, col_last = place()
    channels = hidden_ref.shape[2]
    hidden_ref[...] = given_ref[...]
    edges = (row_first & (tm == 0), row_last & (tm == 3), col_first, col_last)
    edge_copy(hidden_ref, 8, WIDE, (2, 4, 2), (2, 16, 2), edges)
    center = jnp.zeros((1, channels), F32)
    for frame in range(8):
        center = center + jnp.sum(hidden_ref[frame, 2 * WIDE : 6 * WIDE], axis=0, keepdims=True)
    center = center / (8 * 4 * WIDE)
    high = center.astype(BF16).astype(F32)
    low = (center - high).astype(BF16).astype(F32)
    center = high + low
    for frame in range(8):
        cut_ref[frame, 100:101] = high
        cut_ref[frame, 101:102] = low
        cut_ref[frame, 102:104] = jnp.zeros((2, channels), F32)
    for at in range(4):

        @pl.when(tm == at)
        def _(at=at):
            for frame in range(8):
                for row in range(5):
                    first = (at + row) * WIDE
                    cut_ref[frame, row * PITCH : row * PITCH + PITCH] = (
                        hidden_ref[frame, first : first + PITCH] - center
                    )

    for distance, part_ref in enumerate((s0_ref, s1_ref, s2_ref, s3_ref)):
        target = lax.rem(tm + distance, 4)
        parts = [cut_ref[jnp.maximum(2 * target - 4 + g, 0)] for g in range(6)]
        part_ref[...] = jnp.concatenate(parts, axis=0).astype(BF16)


def last_kernel(
    every_ref, s0_ref, s1_ref, s2_ref, s3_ref, far_before_ref, far_wide_ref, gain_ref, shift_ref, far_two_ref,
    offset_two_ref, far_three_ref, offset_three_ref,
    out_ref, act_ref, block_ref, part_ref, sum_ref, mix_ref, piece_ref, before_ref, wide_ref, kernel_two_ref,
    kernel_three_ref, piece_sems, two_sems, three_sems,
):
    tm, row_first, row_last, col_first, col_last = place()
    channels = gain_ref.shape[1]
    pieces = [(ref, piece_ref.at[d]) for d, ref in enumerate((s0_ref, s1_ref, s2_ref, s3_ref))]
    arrivals = fetch([*pieces, (far_before_ref, before_ref), (far_wide_ref, wide_ref)], piece_sems)
    kernels_two = fetch_taps(far_two_ref, kernel_two_ref, two_sems, (0,))
    mean, factor = norm_terms(every_ref[...], gain_ref[...], 4 * 512)
    wait_all(arrivals[:4])
    kernels_two += fetch_taps(far_two_ref, kernel_two_ref, two_sems, (1, 2))
    for source in range(4):
        held = piece_ref[lax.rem(tm + 4 - source, 4)].astype(F32)
        offset = (held[100:101] + held[101:102]) - mean
        for frame in range(6):
            value = held[frame * 104 : frame * 104 + 100] + offset
            act_ref[frame, source * 100 : source * 100 + 100] = norm_silu(value, 0.0, factor, shift_ref[...])
    wait_all(arrivals[4:])
    for frame in range(4):
        for row in range(18):
            own = wide_ref[max(frame - 2, 0), row + 2, 2:22].astype(F32)
            if frame < 2:
                own = jnp.where(tm == 0, own, before_ref[frame, row + 2, 2:22].astype(F32))
            block_ref[frame, row * PITCH : row * PITCH + PITCH] = own
    size = 18 * PITCH
    for p in range(3):
        wait_all(kernels_two[3 * p : 3 * p + 3])
        if p == 0:
            kernels_three = fetch_taps(far_three_ref, kernel_three_ref, three_sems, range(3))
        for pair in range(2):
            for q in range(3):
                rows = []
                for frame in (2 * pair, 2 * pair + 1):
                    start = p * PITCH + q
                    parts = [act_ref[frame + s, start : start + size] for s in range(3)]
                    rows.append(jnp.concatenate(parts, axis=1))
                product = jnp.dot(
                    jnp.concatenate(rows, axis=0).astype(BF16),
                    taps(kernel_two_ref, p, q),
                    preferred_element_type=F32,
                ).reshape(2, size, channels)
                if p + q == 0:
                    product = product + offset_two_ref[...]
                block_ref[2 * pair : 2 * pair + 2] += product
    edge_copy(block_ref, 4, PITCH, (1, 16, 1), (1, 16, 1), (row_first, row_last, col_first, col_last))
    rows = [
        jnp.concatenate([block_ref[frame + s] for s in range(3)], axis=1)
        for frame in range(2)
    ]
    wide = jnp.concatenate(rows, axis=0).astype(BF16)
    out_size = 16 * PITCH
    wait_all(kernels_three)
    for p in range(3):
        for q in range(3):
            part_ref[q, :, 0:size] = jnp.dot(
                wide, taps(kernel_three_ref, p, q), preferred_element_type=F32
            ).reshape(2, size, channels)
        middle = part_ref[1, :, 1 : 1 + size]
        sum_ref[p, 0] = part_ref[0, :, 0:size] + middle + part_ref[2, :, 1 : 1 + size]
        sum_ref[p, 1] = part_ref[0, :, 1 : 1 + size] + middle + part_ref[2, :, 2 : 2 + size]
    for frame in range(2):
        for half in range(channels // 128):
            lanes = slice(half * 128, half * 128 + 128)
            for b in range(2):
                middle = sum_ref[1, b, frame, PITCH : PITCH + out_size, lanes] + offset_three_ref[:, lanes]
                for a in range(2):
                    up = sum_ref[0, b, frame, a * PITCH : a * PITCH + out_size, lanes]
                    down = sum_ref[2, b, frame, (1 + a) * PITCH : (1 + a) * PITCH + out_size, lanes]
                    mix_ref[frame, half, a, pl.ds(b, out_size, stride=2), :] = up + middle + down
            for a in range(2):
                for i in range(16):
                    at = 2 * PITCH * i
                    out_ref[frame, 2 * i + a, :, lanes] = mix_ref[frame, half, a, at : at + 32].astype(BF16)


def run_kernel(body, name, in_specs, out_shape, scratch, flops, limit, *args):
    return pl.pallas_call(
        body,
        name=name,
        out_shape=out_shape,
        in_specs=in_specs,
        out_specs=jax.tree.map(lambda _: VMEM, out_shape),
        scratch_shapes=scratch,
        cost_estimate=pl.CostEstimate(flops=flops, bytes_accessed=8 * 2**20, transcendentals=0),
        compiler_params=pltpu.CompilerParams(vmem_limit_bytes=limit * 2**20),
    )(*args)


def held_taps(channels):
    return pltpu.VMEM((3, 3, 3, channels, channels), BF16)


def strip_call(every, wide, before, strips, gain, shift, kernel, offset):
    channels = wide.shape[3]
    return run_kernel(
        strip_kernel,
        "strip",
        [VMEM] * 9,
        (jax.ShapeDtypeStruct((8, 128), F32), jax.ShapeDtypeStruct((8, 8 * WIDE, channels), F32)),
        [pltpu.VMEM((8, 224, channels), F32)],
        2 * 1408 * 27 * channels * channels,
        24,
        every, wide, before, *strips, gain, shift, kernel, offset,
    )


def cut_call(hidden):
    channels = hidden.shape[2]
    part_shape = jax.ShapeDtypeStruct((624, channels), BF16)
    scratch = [pltpu.VMEM((8, 8 * WIDE, channels), F32), pltpu.VMEM((8, 104, channels), F32)]
    return run_kernel(cut_kernel, "cut", [VMEM], (part_shape,) * 4, scratch, 2**20, 16, hidden)


def last_call(every, parts, before, wide, gain, shift, kernel_two, offset_two, kernel_three, offset_three):
    channels = wide.shape[3]
    macs = 27 * channels * channels
    return run_kernel(
        last_kernel,
        "last",
        [VMEM] + [ANY] * 6 + [VMEM, VMEM, ANY, VMEM, ANY, VMEM],
        jax.ShapeDtypeStruct((2, 32, 32, channels), BF16),
        [
            pltpu.VMEM((6, 408, channels), F32),
            pltpu.VMEM((4, 18 * PITCH, channels), F32),
            pltpu.VMEM((3, 2, 19 * PITCH, channels), F32),
            pltpu.VMEM((3, 2, 2, 18 * PITCH, channels), F32),
            pltpu.VMEM((2, channels // 128, 2, 32 * PITCH, 128), F32),
            pltpu.VMEM((4, 624, channels), BF16),
            pltpu.VMEM((2, 22, WIDE, channels), BF16),
            pltpu.VMEM((2, 22, WIDE, channels), BF16),
            held_taps(channels),
            held_taps(channels),
            pltpu.SemaphoreType.DMA((6,)),
            pltpu.SemaphoreType.DMA((9,)),
            pltpu.SemaphoreType.DMA((9,)),
        ],
        2 * 2160 * macs,
        62,
        every, *parts, before, wide, gain, shift, kernel_two, offset_two, kernel_three, offset_three,
    )


def merged(rows):
    means = jnp.concatenate([row[:, :GROUPS] for row in rows])
    spreads = jnp.concatenate([row[:, GROUPS:] for row in rows])
    mean = jnp.mean(means, axis=0, keepdims=True)
    off = means - mean
    count = 512 * (256 // GROUPS)
    return jnp.concatenate(
        [mean, jnp.sum(spreads, axis=0, keepdims=True) + count * jnp.sum(off * off, axis=0, keepdims=True)],
        axis=1,
    )


def tm_rows(row):
    row = row[:1, :64]
    return [row] + [around(row, "tm", d) for d in (1, 2, 3)]


def repeated(row):
    row = jnp.concatenate([row, row], axis=1)
    peers = lax.axis_size("row") * lax.axis_size("col")
    return jnp.broadcast_to(row, (peers, row.shape[1]))


def exchanged(sent):
    return lax.all_to_all(sent, ("row", "col"), 0, 0, tiled=True)


def moved(value, axis, distance):
    devices = range(lax.axis_size(axis))
    return lax.ppermute(value, axis, [(i, i + distance) for i in devices if i + distance in devices])


def around(value, axis, distance):
    size = lax.axis_size(axis)
    return lax.ppermute(value, axis, [(i, (i + distance) % size) for i in range(size)])


def gathered(latents):
    _, row_first, row_last, col_first, col_last = place()
    left, right = moved(latents[:, :, 13:], "col", 1), moved(latents[:, :, :3], "col", -1)
    row_shape = jax.ShapeDtypeStruct((8, 128), F32)
    x_shape = jax.ShapeDtypeStruct(latents.shape, BF16)
    side_shape = jax.ShapeDtypeStruct((2, 16, 1, latents.shape[3]), BF16)
    row, x, first, last = run_kernel(
        first_kernel, "first", [VMEM], (row_shape, x_shape, side_shape, side_shape), [], 2**20, 8, latents
    )
    row, x, left, right = lax.optimization_barrier((row, x, left, right))
    left = jnp.where(col_first, first, left)
    right = jnp.where(col_last, last, right)
    x = jnp.concatenate([left, x, right], axis=2)
    top, bottom = moved(x[:, 13:], "row", 1), moved(x[:, :3], "row", -1)
    rows = tm_rows(row)
    top = jnp.where(row_first, x[:, :1], top)
    bottom = jnp.where(row_last, x[:, 15:], bottom)
    return merged(rows), jnp.concatenate([top, x, bottom], axis=1)


def strip_of(wide, peer):
    return lax.dynamic_slice_in_dim(wide, 4 * peer, 10, axis=1)


def on_device(
    latents, gain_one, shift_one, kernel_one, offset_one, gain_two, shift_two, kernel_two, offset_two,
    kernel_three, offset_three,
):
    gain_one, shift_one, offset_one, gain_two, shift_two, offset_two, offset_three = (
        v[None] for v in (gain_one, shift_one, offset_one, gain_two, shift_two, offset_two, offset_three)
    )
    tm = lax.axis_index("tm")
    row, wide = gathered(latents)
    before = around(wide.reshape(44, WIDE, -1), "tm", 1).reshape(wide.shape)
    strips = [around(strip_of(wide, (tm + d) % 4), "tm", d) for d in (2, 3)]
    every = exchanged(repeated(row))
    row, hidden = strip_call(every, wide, before, strips, gain_one, shift_one, kernel_one, offset_one)
    sent = repeated(merged(tm_rows(row)))
    parts = cut_call(hidden)
    parts = [parts[0]] + [around(parts[d], "tm", d) for d in (1, 2, 3)]
    every = exchanged(sent)
    return last_call(
        every, parts, before, wide, gain_two, shift_two, kernel_two, offset_two, kernel_three, offset_three
    )


def solution(mesh):
    return jax.shard_map(
        on_device,
        mesh=mesh,
        in_specs=(P("tm", "row", "col", None), P(), P(), P(), P(), P(), P(), P(), P(), P(), P()),
        out_specs=P("tm", "row", "col", None),
        check_vma=False,
    )
```
